32 devices in a mesh: seq: 8 (over y, x, core), tensor: 4 (over z).
Axes of the slice: x: 2, y: 2, z: 4, core: 2. Of those that a mesh axis runs over, the one named last changes fastest.
Arguments:
- tokens: bfloat16 [6144, 2048], P('seq'), may hold values from -6 to 6
- norm_gain: float32 [2048], replicated, may hold values from 0.1 to 1.9
- query_weight: bfloat16 [2048, 2048], P(None, 'tensor'), may hold values from -0.125 to 0.125
- key_value_matrix: bfloat16 [2048, 4, 128], replicated, may hold values from -0.125 to 0.125
- out_weight: bfloat16 [2048, 2048], replicated, may hold values from -0.125 to 0.125
- cache_pages: bfloat16 [512, 4, 128, 128], P('seq'), may hold values from -180 to 180, as said below
- page_table: int32 [8, 64], replicated, may hold values from 0 to 511, as said below
- request_lengths: int32 [40], replicated, may hold values from 1 to 764, as said below
- request_groups: int32 [40], replicated, may hold values from 0 to 7
Outputs:
- projected: bfloat16 [6144, 2048], P('seq', 'tensor')
The draws below stay inside these ranges and needn't reach their ends.
Inputs may be any that keep to these rules, and one draw needn't show every extreme that they name: `page_table`: every page id appears once. Of the last 16 entries of each row, exactly 2 lie in each block of 64 consecutive ids, the pages held by one seq device. `request_lengths`: the lengths of the 5 requests of one seq device sum to at most 768, and to exactly 768 on at least one device. `cache_pages`: keys in the first 64 entries of the last dimension, values in the rest.
All inputs are finite; a program needn't handle non-finite values.
Results may differ from the reference program's by a relative error of at most 0.012.
The reference program's roundings to bfloat16 on the way count: a program that leaves them out, or rounds other values in their place, can miss the bound.
Values may be sent and summed in bfloat16 or wider, within the bound.
A program may use at most 128 MiB of HBM per device.

```python
import math
import jax
import jax.numpy as jnp
import numpy as np
from jax import lax

MODEL_WIDTH = 2048
QUERY_HEADS = 32
KEY_VALUE_HEADS = 4
HEAD_SIZE = 64
WINDOW_LENGTH = 2048
PAGE_LENGTH = 128
TOKEN_CAPACITY = 768
DEVICE_REQUESTS = 5
PPG = 64
WP = 16
GROUPS = 8
PAGES_DEV = 64
PAGE_TOTAL = 512
TPO = 2
REQS = 40
ROWS = 6144
N_SEQ = 8


def draw_cache_pages(key, part):
    base_key = jax.random.fold_in(key, 101)
    page_dimensions = (PAGE_TOTAL, KEY_VALUE_HEADS, PAGE_LENGTH, 2 * HEAD_SIZE)
    entries = jnp.clip(jax.random.normal(base_key, page_dimensions, jnp.float32), -5.0, 5.0)
    return entries.astype(jnp.bfloat16)


def draw_page_table(key, part):
    owner_key = jax.random.fold_in(key, 201)
    slot_key = jax.random.fold_in(key, 202)
    tail_scores = jax.random.randint(owner_key, (GROUPS, WP), 0, 1 << 20, dtype=jnp.int32) * WP + lax.broadcasted_iota(jnp.int32, (GROUPS, WP), 1)
    tail_order = jnp.argsort(tail_scores, axis=1).astype(jnp.int32)
    slot_scores = jax.random.randint(slot_key, (N_SEQ, PAGES_DEV), 0, 1 << 20, dtype=jnp.int32) * PAGES_DEV + lax.broadcasted_iota(jnp.int32, (N_SEQ, PAGES_DEV), 1)
    slot_order = jnp.argsort(slot_scores, axis=1).astype(jnp.int32)
    group_ids = lax.broadcasted_iota(jnp.int32, (GROUPS, WP), 0)
    tail_owner = tail_order // TPO
    tail_slot = group_ids * TPO + tail_order % TPO
    tail_ids = tail_owner * PAGES_DEV + slot_order[tail_owner, tail_slot]
    rest_count = PPG - WP
    spare_slots = PAGES_DEV - WP
    flat_index = lax.broadcasted_iota(jnp.int32, (GROUPS, rest_count), 0) * rest_count + lax.broadcasted_iota(jnp.int32, (GROUPS, rest_count), 1)
    rest_owner = flat_index // spare_slots
    rest_slot = WP + flat_index % spare_slots
    rest_ids = rest_owner * PAGES_DEV + slot_order[rest_owner, rest_slot]
    return jnp.concatenate([rest_ids, tail_ids], axis=1).astype(jnp.int32)


def draw_request_lengths(key, part):
    full_key = jax.random.fold_in(key, 301)
    load_key = jax.random.fold_in(key, 302)
    share_key = jax.random.fold_in(key, 303)
    full_device = jax.random.randint(full_key, (), 0, N_SEQ, dtype=jnp.int32)
    device_loads = jax.random.randint(load_key, (N_SEQ,), 2 * TOKEN_CAPACITY // 5, TOKEN_CAPACITY + 1, dtype=jnp.int32)
    device_loads = jnp.where(lax.iota(jnp.int32, N_SEQ) == full_device, TOKEN_CAPACITY, device_loads)
    shares = jax.random.randint(share_key, (N_SEQ, DEVICE_REQUESTS), 1, 17, dtype=jnp.int32)
    share_total = jnp.sum(shares, axis=1, keepdims=True).astype(jnp.int32)
    spare_rows = (device_loads - DEVICE_REQUESTS)[:, None]
    lengths = 1 + spare_rows * shares // share_total
    leftover = device_loads - jnp.sum(lengths, axis=1).astype(jnp.int32)
    last_slot = lax.broadcasted_iota(jnp.int32, (N_SEQ, DEVICE_REQUESTS), 1) == DEVICE_REQUESTS - 1
    lengths = jnp.where(last_slot, lengths + leftover[:, None], lengths)
    full_row = lax.broadcasted_iota(jnp.int32, (N_SEQ, DEVICE_REQUESTS), 0) == full_device
    single = jnp.where(last_slot, TOKEN_CAPACITY - DEVICE_REQUESTS + 1, 1).astype(jnp.int32)
    lengths = jnp.where(full_row, single, lengths)
    return lengths.reshape(N_SEQ * DEVICE_REQUESTS).astype(jnp.int32)


def touch_ends(result, own_key, least, high):
    longest = result.shape.index(max(result.shape))
    spots = []
    for shift in (0, 1):
        where = [jax.random.randint(jax.random.fold_in(own_key, axis), (), 0, length) for axis, length in enumerate(result.shape)]
        where[longest] = (where[longest] + shift) % result.shape[longest]
        spots.append(tuple(where))
    return result.at[spots[0]].set(least).at[spots[1]].set(high)


def steps_of(key, dims, shards, least, top_value):
    loudness = 1.0
    for dim, blocks in shards:
        steps = jax.random.uniform(jax.random.fold_in(jax.random.fold_in(key, 6), dim), (blocks,), jnp.float32, least / len(shards), top_value / len(shards))
        loudness = loudness * jnp.repeat(jnp.exp(steps), dims[dim] // blocks).reshape((-1,) + (1,) * (len(dims) - 1 - dim))
    return loudness


def rank_bounds(count, slope):
    weights = [(1 << 20) // math.isqrt(standing ** slope) + 1 for standing in range(1, count + 1)]
    width = 1 + sum(weights) // (1 << 30)
    return np.cumsum(np.array([max(1, weight // width) for weight in weights]))


def ranked_ids(key, extent, amount, skew):
    grid = rank_bounds(amount, skew)
    ticket = jax.random.randint(jax.random.fold_in(key, 1), extent, 0, int(grid[amount - 1]))
    grade = jnp.searchsorted(jnp.asarray(grid, jnp.int32), ticket, side="right")
    return jax.random.permutation(jax.random.fold_in(key, 2), amount)[grade].astype(jnp.int32)


def normal_values(own_key, shape, width, bound, cuts=(), kind=jnp.bfloat16):
    values = jax.random.normal(own_key, shape, jnp.float32) * width
    if len(cuts) > 0:
        values = steps_of(own_key, shape, cuts, -0.22, 0.18) * values
    return jnp.clip(values, min=-bound, max=bound).astype(kind)


def setup_inputs(seed: int = 0) -> dict:
    key_list = jax.random.split(jax.random.key(seed), 10)
    tokens = normal_values(key_list[0], (ROWS, MODEL_WIDTH), 1.0, 6.0, ((0, 8),))
    norm_gain = jnp.clip(1.0 + 0.18 * jax.random.normal(key_list[1], (MODEL_WIDTH,), jnp.float32), 0.1, 1.9)
    query_weight = normal_values(key_list[2], (MODEL_WIDTH, QUERY_HEADS * HEAD_SIZE), MODEL_WIDTH ** -0.5, 0.125, ((1, 4),))
    key_value_matrix = normal_values(key_list[3], (MODEL_WIDTH, KEY_VALUE_HEADS, 2 * HEAD_SIZE), MODEL_WIDTH ** -0.5, 0.125)
    out_weight = normal_values(key_list[4], (QUERY_HEADS * HEAD_SIZE, MODEL_WIDTH), (QUERY_HEADS * HEAD_SIZE) ** -0.5, 0.125)
    cache_pages = draw_cache_pages(jax.random.fold_in(key_list[9], 71), 0)
    page_table = draw_page_table(jax.random.fold_in(key_list[9], 71), 0)
    request_lengths = draw_request_lengths(jax.random.fold_in(key_list[9], 71), 0)
    request_groups = touch_ends(ranked_ids(key_list[8], (REQS,), GROUPS, 2), jax.random.fold_in(key_list[8], 3), 0, GROUPS - 1).astype(jnp.int32)
    return dict(tokens=tokens, norm_gain=norm_gain, query_weight=query_weight, key_value_matrix=key_value_matrix, out_weight=out_weight, cache_pages=cache_pages, page_table=page_table, request_lengths=request_lengths, request_groups=request_groups)


MASKED_SCORE = -1e+30

def normalize(tokens, norm_gain):
    widened = tokens.astype(jnp.float32)
    factor = lax.rsqrt(lax.optimization_barrier(jnp.mean(widened * widened, axis=-1, keepdims=True)) + 1e-05)
    return (widened * factor * norm_gain).astype(jnp.bfloat16)

def row_layout(lengths, row_total_count):
    lengths = lengths.astype(jnp.int32)
    request_ends = jnp.cumsum(lengths).astype(jnp.int32)
    starts = request_ends - lengths
    slot_ids = lax.iota(jnp.int32, row_total_count)
    row_request = lax.optimization_barrier(jnp.sum((slot_ids[:, None] >= request_ends[None, :]).astype(jnp.int32), axis=1)).astype(jnp.int32)
    row_live = slot_ids < request_ends[-1]
    choose = row_request[:, None] == lax.iota(jnp.int32, lengths.shape[0])[None, :]
    begins = lax.optimization_barrier(jnp.sum(jnp.where(choose, starts[None, :], 0), axis=1)).astype(jnp.int32)
    return (row_request, row_live, slot_ids - begins)

def reference(tokens, norm_gain, query_weight, key_value_matrix, out_weight, cache_pages, page_table, request_lengths, request_groups):
    score_scale = HEAD_SIZE ** (-0.5)
    query_group_width = QUERY_HEADS // KEY_VALUE_HEADS
    tail_ids = page_table[:, PPG - WP:]
    flattened_weight = key_value_matrix.reshape(MODEL_WIDTH, KEY_VALUE_HEADS * 2 * HEAD_SIZE)

    def one_device(inputs):
        device_tokens, lengths, groups_here = inputs
        normed = normalize(device_tokens, norm_gain)
        query_rows = jnp.dot(normed, query_weight, preferred_element_type=jnp.float32).astype(jnp.bfloat16)
        new_token_rows = jnp.dot(normed, flattened_weight, preferred_element_type=jnp.float32).astype(jnp.bfloat16)
        new_rows_widened = new_token_rows.astype(jnp.float32).reshape(TOKEN_CAPACITY, KEY_VALUE_HEADS, 2 * HEAD_SIZE)
        row_request, row_live, row_position = row_layout(lengths, TOKEN_CAPACITY)
        visible_pages = cache_pages[tail_ids[groups_here]]
        window_widened = jnp.transpose(visible_pages, (0, 2, 1, 3, 4)).reshape(DEVICE_REQUESTS, KEY_VALUE_HEADS, WINDOW_LENGTH, 2 * HEAD_SIZE).astype(jnp.float32)
        query_widened = query_rows.astype(jnp.float32).reshape(TOKEN_CAPACITY // 16, 16, KEY_VALUE_HEADS, query_group_width, HEAD_SIZE)
        column = lax.iota(jnp.int32, TOKEN_CAPACITY)
        offsets = lax.iota(jnp.int32, WINDOW_LENGTH)

        def one_block(block_inputs):
            block_query, block_request, block_live, block_position, block_rows = block_inputs
            picked = window_widened[jnp.minimum(block_request, DEVICE_REQUESTS - 1)]
            prefix_scores = jnp.einsum('rkgd,rkmd->rkgm', block_query, picked[..., :HEAD_SIZE]) * score_scale
            suffix_scores = jnp.einsum('rkgd,ckd->rkgc', block_query, new_rows_widened[..., :HEAD_SIZE]) * score_scale
            prefix_mask = (block_live[:, None] & (offsets[None, :] >= block_position[:, None] + 1))[:, None, None, :]
            suffix_mask = ((row_request[None, :] == block_request[:, None]) & block_live[:, None] & (column[None, :] <= block_rows[:, None]) & (block_rows[:, None] - column[None, :] < WINDOW_LENGTH))[:, None, None, :]
            row_top = jnp.maximum(lax.optimization_barrier(jnp.max(jnp.where(prefix_mask, prefix_scores, MASKED_SCORE), axis=-1)), lax.optimization_barrier(jnp.max(jnp.where(suffix_mask, suffix_scores, MASKED_SCORE), axis=-1)))
            prefix_raw = jnp.where(prefix_mask, jnp.exp(prefix_scores - row_top[..., None]), 0.0)
            suffix_raw = jnp.where(suffix_mask, jnp.exp(suffix_scores - row_top[..., None]), 0.0)
            row_total = lax.optimization_barrier(jnp.sum(prefix_raw, axis=-1)) + lax.optimization_barrier(jnp.sum(suffix_raw, axis=-1))
            prefix_weights = lax.optimization_barrier(prefix_raw.astype(jnp.bfloat16)).astype(jnp.float32)
            suffix_weights = lax.optimization_barrier(suffix_raw.astype(jnp.bfloat16)).astype(jnp.float32)
            weighted = jnp.einsum('rkgm,rkmd->rkgd', prefix_weights, picked[..., HEAD_SIZE:])
            weighted = weighted + jnp.einsum('rkgc,ckd->rkgd', suffix_weights, new_rows_widened[..., HEAD_SIZE:])
            safe_total = jnp.where(block_live[:, None, None], row_total, 1.0)
            attended = jnp.where(block_live[:, None, None, None], weighted / safe_total[..., None], 0.0)
            return attended.astype(jnp.bfloat16).reshape(16, QUERY_HEADS * HEAD_SIZE)
        blocks = (query_widened, row_request.reshape(-1, 16), row_live.reshape(-1, 16), row_position.reshape(-1, 16), column.reshape(-1, 16))
        attended = lax.map(one_block, blocks).reshape(TOKEN_CAPACITY, QUERY_HEADS * HEAD_SIZE)
        return jnp.dot(attended, out_weight, preferred_element_type=jnp.float32).astype(jnp.bfloat16)
    outputs = lax.map(one_device, (tokens.reshape(N_SEQ, TOKEN_CAPACITY, MODEL_WIDTH), request_lengths.reshape(N_SEQ, DEVICE_REQUESTS), request_groups.reshape(N_SEQ, DEVICE_REQUESTS)))
    return outputs.reshape(N_SEQ * TOKEN_CAPACITY, MODEL_WIDTH)
```

```python
import functools
import math

import jax
import jax.numpy as jnp
from jax import lax
from jax.experimental import pallas as pl
from jax.experimental.pallas import tpu as pltpu
from jax.sharding import PartitionSpec as P

QUERY_HEADS = 32
KEY_VALUE_HEADS = 4
HEAD_SIZE = 64
WINDOW_LENGTH = 2048
DEVICE_REQUESTS = 5
PPG = 64
WP = 16
PAGE = 128
VROWS = 80
MASKED_SCORE = -1e30
SCALE = HEAD_SIZE ** (-0.5) * math.log2(math.e)


def normalize(tokens, norm_gain):
    widened = tokens.astype(jnp.float32)
    factor = lax.rsqrt(jnp.mean(widened * widened, axis=-1, keepdims=True) + 1e-05)
    return (widened * factor * norm_gain).astype(jnp.bfloat16)


def lookup_rows(table, wanted):
    matches = wanted[:, None] == lax.iota(jnp.int32, table.shape[0])[None, :]
    return jnp.sum(jnp.where(matches[:, :, None], table[None, :, :], 0), axis=1)


def pack_kernel(count, slot_ref, cache_ref, out_ref, sems):
    for i in range(count):
        pltpu.make_async_copy(
            cache_ref.at[slot_ref[i], slot_ref[count]], out_ref.at[i], sems.at[i]
        ).start()
    for i in range(count):
        pltpu.make_async_copy(cache_ref.at[0, 0], out_ref.at[i], sems.at[i]).wait()


def attention_kernel(
    rows_per_block, bounds_ref, page_ref, pages_ref, fresh_ref, q_ref, out_ref, kv, vt
):
    block_count, _, width = q_ref.shape
    fresh_count = fresh_ref.shape[0]
    prefix_pages = DEVICE_REQUESTS * WP
    vt[:, HEAD_SIZE:, :] = jnp.ones((vt.shape[0], VROWS - HEAD_SIZE, PAGE), jnp.bfloat16)
    out_ref[...] = jnp.zeros_like(out_ref)

    def place(slot, page):
        kv[slot] = page
        vt[slot, :HEAD_SIZE, :] = jnp.transpose(page)[HEAD_SIZE:]

    def fill(i, carry):
        place(i, pages_ref[page_ref[i]])
        return carry

    lax.fori_loop(0, prefix_pages, fill, 0, unroll=4)
    for i in range(fresh_count):
        place(prefix_pages + i, fresh_ref[i])

    key_index = lax.broadcasted_iota(jnp.int32, (PAGE, width), 0)
    lane_row = lax.broadcasted_iota(jnp.int32, (1, width), 1) % rows_per_block

    def group(slots, masks, query, top, total):
        scores = []
        for slot, mask in zip(slots, masks):
            one = jnp.dot(kv[slot], query, preferred_element_type=jnp.float32) * SCALE
            scores.append(one if mask is None else jnp.where(mask, one, MASKED_SCORE))
        peak = functools.reduce(jnp.maximum, scores)
        peak = jnp.max(peak, axis=0, keepdims=True)
        new_top = peak if top is None else jnp.maximum(top, peak)
        weights = jnp.concatenate(
            [jnp.exp2(one - new_top).astype(jnp.bfloat16) for one in scores], axis=0
        )
        values = jnp.concatenate([vt[slot] for slot in slots], axis=1)
        added = jnp.dot(values, weights, preferred_element_type=jnp.float32)
        if total is not None:
            added = added + total * jnp.exp2(top - new_top)
        return new_top, added

    def one_item(request, block):
        first_row = block * rows_per_block
        start = bounds_ref[request]
        end = bounds_ref[DEVICE_REQUESTS + request]
        query = q_ref[block]
        row = lane_row + first_row
        position = row - start
        first_fresh = start // PAGE
        last_fresh = first_row // PAGE
        first_page = (jnp.maximum(first_row - start, 0) + 1) // PAGE
        base = request * WP
        inside = 14 - first_page
        several = last_fresh > first_fresh

        def plain(u):
            wanted = prefix_pages + first_fresh + 1 + (u - inside)
            return jnp.where(u < inside, base + first_page + 2 + u, wanted)

        count = inside + jnp.maximum(last_fresh - first_fresh - 1, 0)
        slots = [
            base + first_page,
            base + first_page + 1,
            prefix_pages + first_fresh,
            prefix_pages + last_fresh,
            plain(12),
            jnp.where(count > 13, plain(13), base),
        ]
        fresh_low = start - first_fresh * PAGE
        last_high = jnp.where(several, row - last_fresh * PAGE, -1)
        masks = [
            key_index > position - first_page * PAGE,
            key_index > position - (first_page + 1) * PAGE,
            (key_index <= row - first_fresh * PAGE) & (key_index >= fresh_low),
            key_index <= last_high,
            None,
            key_index < jnp.where(count > 13, PAGE, 0),
        ]
        top, total = group(slots, masks, query, None, None)
        for part in range(2):
            slots = [plain(part * 6 + u) for u in range(6)]
            top, total = group(slots, [None] * 6, query, top, total)
        result = total[:HEAD_SIZE] / total[HEAD_SIZE : HEAD_SIZE + 1]
        mine = (row >= start) & (row < end)
        out_ref[block] = jnp.where(
            mine, result, out_ref[block].astype(jnp.float32)
        ).astype(jnp.bfloat16)
        return block

    def one_block(block, carry):
        first_row = block * rows_per_block
        first = 0
        last = -1
        for r in range(DEVICE_REQUESTS):
            first = first + (bounds_ref[DEVICE_REQUESTS + r] <= first_row).astype(jnp.int32)
            last = last + (bounds_ref[r] < first_row + rows_per_block).astype(jnp.int32)
        lax.fori_loop(first, last + 1, one_item, block)
        return carry

    lax.fori_loop(0, block_count, one_block, 0)


def body(
    tokens,
    norm_gain,
    query_weight,
    key_value_matrix,
    out_weight,
    cache_pages,
    page_table,
    request_lengths,
    request_groups,
):
    seq_count = lax.axis_size("seq")
    seq_index = lax.axis_index("seq")
    tensor_index = lax.axis_index("tensor")
    tensor_count = lax.axis_size("tensor")
    row_count = tokens.shape[0]
    heads = query_weight.shape[1] // HEAD_SIZE
    key_value_head = tensor_index * heads // (QUERY_HEADS // KEY_VALUE_HEADS)
    group_count = page_table.shape[0]
    per_owner = WP // seq_count
    pages_here = cache_pages.shape[0]
    send_count = group_count * per_owner

    tail_ids = page_table[:, PPG - WP :]
    holder = tail_ids // pages_here
    local_slot = tail_ids % pages_here
    earlier = lax.iota(jnp.int32, WP)[:, None] > lax.iota(jnp.int32, WP)[None, :]
    same_owner = holder[:, :, None] == holder[:, None, :]
    tail_rank = jnp.sum((same_owner & earlier[None, :, :]).astype(jnp.int32), axis=2)
    tail_hit = (holder == seq_index)[:, :, None] & (
        tail_rank[:, :, None] == lax.iota(jnp.int32, per_owner)[None, None, :]
    )
    tail_pick = jnp.sum(jnp.where(tail_hit, local_slot[:, :, None], 0), axis=1).reshape(-1)
    packed = pl.pallas_call(
        functools.partial(pack_kernel, send_count),
        out_shape=jax.ShapeDtypeStruct((send_count, PAGE, 2 * HEAD_SIZE), jnp.bfloat16),
        in_specs=[
            pl.BlockSpec(memory_space=pltpu.SMEM),
            pl.BlockSpec(memory_space=pl.ANY),
        ],
        out_specs=pl.BlockSpec(memory_space=pl.ANY),
        scratch_shapes=[pltpu.SemaphoreType.DMA((send_count,))],
        name="pack_pages",
    )(jnp.concatenate([tail_pick, key_value_head[None].astype(jnp.int32)]), cache_pages)
    gathered = lax.all_gather(packed, "seq", axis=0, tiled=True)

    normed = normalize(tokens, norm_gain)
    query_rows = jnp.dot(normed, query_weight, preferred_element_type=jnp.float32).astype(
        jnp.bfloat16
    )
    head_weight = lax.dynamic_index_in_dim(key_value_matrix, key_value_head, 1, keepdims=False)
    fresh = jnp.dot(normed, head_weight, preferred_element_type=jnp.float32).astype(jnp.bfloat16)
    fresh = fresh.reshape(row_count // PAGE, PAGE, 2 * HEAD_SIZE)
    rows_per_block = min(PAGE, 256 // heads)
    block_count = row_count // rows_per_block
    width = heads * rows_per_block
    query = query_rows.reshape(block_count, rows_per_block, heads, HEAD_SIZE)
    query = jnp.transpose(query, (0, 3, 2, 1)).reshape(block_count, HEAD_SIZE, width)
    query = jnp.concatenate([query, jnp.zeros_like(query)], axis=1)

    lengths = lax.dynamic_slice_in_dim(
        request_lengths, seq_index * DEVICE_REQUESTS, DEVICE_REQUESTS
    )
    groups = lax.dynamic_slice_in_dim(
        request_groups, seq_index * DEVICE_REQUESTS, DEVICE_REQUESTS
    )
    ends = jnp.cumsum(lengths)
    bounds = jnp.concatenate([ends - lengths, ends])
    where_from = (
        lookup_rows(holder, groups) * send_count
        + groups[:, None] * per_owner
        + lookup_rows(tail_rank, groups)
    ).reshape(-1)
    slots = DEVICE_REQUESTS * WP + row_count // PAGE
    attended = pl.pallas_call(
        functools.partial(attention_kernel, rows_per_block),
        out_shape=jax.ShapeDtypeStruct((block_count, HEAD_SIZE, width), jnp.bfloat16),
        in_specs=[pl.BlockSpec(memory_space=pltpu.SMEM)] * 2
        + [pl.BlockSpec(memory_space=pltpu.VMEM)] * 3,
        out_specs=pl.BlockSpec(memory_space=pltpu.VMEM),
        scratch_shapes=[
            pltpu.VMEM((slots, PAGE, 2 * HEAD_SIZE), jnp.bfloat16),
            pltpu.VMEM((slots, VROWS, PAGE), jnp.bfloat16),
        ],
        compiler_params=pltpu.CompilerParams(vmem_limit_bytes=40 * 1024 * 1024),
        name="attend",
    )(bounds, where_from, gathered, fresh, query)
    attended = attended.reshape(block_count, HEAD_SIZE, heads, rows_per_block)
    attended = jnp.transpose(attended, (0, 3, 2, 1)).reshape(row_count, heads * HEAD_SIZE)
    everything = lax.all_gather(attended, "tensor", axis=1, tiled=True)
    columns = out_weight.shape[1] // tensor_count
    my_columns = lax.dynamic_slice_in_dim(out_weight, tensor_index * columns, columns, 1)
    return jnp.dot(everything, my_columns, preferred_element_type=jnp.float32).astype(jnp.bfloat16)


def solution(mesh):
    return jax.shard_map(
        body,
        mesh=mesh,
        in_specs=(
            P("seq", None),
            P(),
            P(None, "tensor"),
            P(),
            P(),
            P("seq", None, None, None),
            P(),
            P(),
            P(),
        ),
        out_specs=P("seq", "tensor"),
        check_vma=False,
    )
```

```python
import functools
import math

import jax
import jax.numpy as jnp
from jax import lax
from jax.experimental import pallas as pl
from jax.experimental.pallas import tpu as pltpu
from jax.sharding import PartitionSpec as P

QUERY_HEADS = 32
KEY_VALUE_HEADS = 4
HEAD_SIZE = 64
WINDOW_LENGTH = 2048
DEVICE_REQUESTS = 5
PPG = 64
WP = 16
PAGE = 128
VROWS = 80
MASKED_SCORE = -1e30
SCALE = HEAD_SIZE ** (-0.5) * math.log2(math.e)


def normalize(tokens, norm_gain):
    widened = tokens.astype(jnp.float32)
    factor = lax.rsqrt(jnp.mean(widened * widened, axis=-1, keepdims=True) + 1e-05)
    return (widened * factor * norm_gain).astype(jnp.bfloat16)


def lookup_rows(table, wanted):
    matches = wanted[:, None] == lax.iota(jnp.int32, table.shape[0])[None, :]
    return jnp.sum(jnp.where(matches[:, :, None], table[None, :, :], 0), axis=1)


def pack_kernel(count, slot_ref, cache_ref, out_ref, sems):
    for i in range(count):
        pltpu.make_async_copy(
            cache_ref.at[slot_ref[i], slot_ref[count]], out_ref.at[i], sems.at[i]
        ).start()
    for i in range(count):
        pltpu.make_async_copy(cache_ref.at[0, 0], out_ref.at[i], sems.at[i]).wait()


def attention_kernel(
    rows_per_block, bounds_ref, page_ref, pages_ref, fresh_ref, q_ref, out_ref, kv, vt, held
):
    block_count, _, width = q_ref.shape
    fresh_count = fresh_ref.shape[0]
    prefix_pages = DEVICE_REQUESTS * WP
    vt[:, HEAD_SIZE:, :] = jnp.ones((vt.shape[0], VROWS - HEAD_SIZE, PAGE), jnp.bfloat16)

    def place(slot, page):
        kv[slot] = page
        vt[slot, :HEAD_SIZE, :] = jnp.transpose(page)[HEAD_SIZE:]

    def fill(i, carry):
        place(i, pages_ref[page_ref[i]])
        return carry

    lax.fori_loop(0, prefix_pages, fill, 0, unroll=4)
    for i in range(fresh_count):
        place(prefix_pages + i, fresh_ref[i])

    key_index = lax.broadcasted_iota(jnp.int32, (PAGE, width), 0)
    lane_row = lax.broadcasted_iota(jnp.int32, (1, width), 1) % rows_per_block

    def group(slots, masks, query, top, total):
        scores = []
        for slot, mask in zip(slots, masks):
            one = jnp.dot(kv[slot], query, preferred_element_type=jnp.float32) * SCALE
            scores.append(one if mask is None else jnp.where(mask, one, MASKED_SCORE))
        peak = functools.reduce(jnp.maximum, scores)
        peak = jnp.max(peak, axis=0, keepdims=True)
        new_top = peak if top is None else jnp.maximum(top, peak)
        weights = jnp.concatenate(
            [jnp.exp2(one - new_top).astype(jnp.bfloat16) for one in scores], axis=0
        )
        values = jnp.concatenate([vt[slot] for slot in slots], axis=1)
        added = jnp.dot(values, weights, preferred_element_type=jnp.float32)
        if total is not None:
            added = added + total * jnp.exp2(top - new_top)
        return new_top, added

    def one_item(request, block):
        first_row = block * rows_per_block
        start = bounds_ref[request]
        end = bounds_ref[DEVICE_REQUESTS + request]
        query = q_ref[block]
        row = lane_row + first_row
        position = row - start
        first_fresh = start // PAGE
        last_fresh = first_row // PAGE
        first_page = (jnp.maximum(first_row - start, 0) + 1) // PAGE
        base = request * WP
        inside = 14 - first_page
        several = last_fresh > first_fresh

        def plain(u):
            wanted = prefix_pages + first_fresh + 1 + (u - inside)
            return jnp.where(u < inside, base + first_page + 2 + u, wanted)

        count = inside + jnp.maximum(last_fresh - first_fresh - 1, 0)
        slots = [
            base + first_page,
            base + first_page + 1,
            prefix_pages + first_fresh,
            prefix_pages + last_fresh,
            plain(12),
            jnp.where(count > 13, plain(13), base),
        ]
        fresh_low = start - first_fresh * PAGE
        last_high = jnp.where(several, row - last_fresh * PAGE, -1)
        masks = [
            key_index > position - first_page * PAGE,
            key_index > position - (first_page + 1) * PAGE,
            (key_index <= row - first_fresh * PAGE) & (key_index >= fresh_low),
            key_index <= last_high,
            None,
            key_index < jnp.where(count > 13, PAGE, 0),
        ]
        top, total = group(slots, masks, query, None, None)
        for part in range(2):
            slots = [plain(part * 6 + u) for u in range(6)]
            top, total = group(slots, [None] * 6, query, top, total)
        result = total[:HEAD_SIZE] / total[HEAD_SIZE : HEAD_SIZE + 1]
        mine = (row >= start) & (row < end)
        held[...] = jnp.where(mine, result, held[...])
        return block

    def one_block(block, carry):
        first_row = block * rows_per_block
        first = 0
        last = -1
        for r in range(DEVICE_REQUESTS):
            first = first + (bounds_ref[DEVICE_REQUESTS + r] <= first_row).astype(jnp.int32)
            last = last + (bounds_ref[r] < first_row + rows_per_block).astype(jnp.int32)
        held[...] = jnp.zeros_like(held)
        lax.fori_loop(first, last + 1, one_item, block)
        turned = jnp.transpose(held[...])
        heads = width // rows_per_block
        pieces = [turned[h * rows_per_block : (h + 1) * rows_per_block] for h in range(heads)]
        out_ref[block] = jnp.concatenate(pieces, axis=1).astype(jnp.bfloat16)
        return carry

    lax.fori_loop(0, block_count, one_block, 0)


def body(
    tokens,
    norm_gain,
    query_weight,
    key_value_matrix,
    out_weight,
    cache_pages,
    page_table,
    request_lengths,
    request_groups,
):
    seq_count = lax.axis_size("seq")
    seq_index = lax.axis_index("seq")
    tensor_index = lax.axis_index("tensor")
    tensor_count = lax.axis_size("tensor")
    row_count = tokens.shape[0]
    heads = query_weight.shape[1] // HEAD_SIZE
    key_value_head = tensor_index * heads // (QUERY_HEADS // KEY_VALUE_HEADS)
    group_count = page_table.shape[0]
    per_owner = WP // seq_count
    pages_here = cache_pages.shape[0]
    send_count = group_count * per_owner

    tail_ids = page_table[:, PPG - WP :]
    holder = tail_ids // pages_here
    local_slot = tail_ids % pages_here
    earlier = lax.iota(jnp.int32, WP)[:, None] > lax.iota(jnp.int32, WP)[None, :]
    same_owner = holder[:, :, None] == holder[:, None, :]
    tail_rank = jnp.sum((same_owner & earlier[None, :, :]).astype(jnp.int32), axis=2)
    tail_hit = (holder == seq_index)[:, :, None] & (
        tail_rank[:, :, None] == lax.iota(jnp.int32, per_owner)[None, None, :]
    )
    tail_pick = jnp.sum(jnp.where(tail_hit, local_slot[:, :, None], 0), axis=1).reshape(-1)
    packed = pl.pallas_call(
        functools.partial(pack_kernel, send_count),
        out_shape=jax.ShapeDtypeStruct((send_count, PAGE, 2 * HEAD_SIZE), jnp.bfloat16),
        in_specs=[
            pl.BlockSpec(memory_space=pltpu.SMEM),
            pl.BlockSpec(memory_space=pl.ANY),
        ],
        out_specs=pl.BlockSpec(memory_space=pltpu.VMEM),
        scratch_shapes=[pltpu.SemaphoreType.DMA((send_count,))],
        name="pack_pages",
    )(jnp.concatenate([tail_pick, key_value_head[None].astype(jnp.int32)]), cache_pages)
    gathered = lax.all_gather(packed, "seq", axis=0, tiled=True)

    normed = normalize(tokens, norm_gain)
    query_rows = jnp.dot(normed, query_weight, preferred_element_type=jnp.float32).astype(
        jnp.bfloat16
    )
    head_weight = lax.dynamic_index_in_dim(key_value_matrix, key_value_head, 1, keepdims=False)
    fresh = jnp.dot(normed, head_weight, preferred_element_type=jnp.float32).astype(jnp.bfloat16)
    fresh = fresh.reshape(row_count // PAGE, PAGE, 2 * HEAD_SIZE)
    rows_per_block = min(PAGE, 256 // heads)
    block_count = row_count // rows_per_block
    width = heads * rows_per_block
    query = query_rows.reshape(block_count, rows_per_block, heads, HEAD_SIZE)
    query = jnp.transpose(query, (0, 3, 2, 1)).reshape(block_count, HEAD_SIZE, width)
    query = jnp.concatenate([query, jnp.zeros_like(query)], axis=1)

    lengths = lax.dynamic_slice_in_dim(
        request_lengths, seq_index * DEVICE_REQUESTS, DEVICE_REQUESTS
    )
    groups = lax.dynamic_slice_in_dim(
        request_groups, seq_index * DEVICE_REQUESTS, DEVICE_REQUESTS
    )
    ends = jnp.cumsum(lengths)
    bounds = jnp.concatenate([ends - lengths, ends])
    where_from = (
        lookup_rows(holder, groups) * send_count
        + groups[:, None] * per_owner
        + lookup_rows(tail_rank, groups)
    ).reshape(-1)
    slots = DEVICE_REQUESTS * WP + row_count // PAGE
    attended = pl.pallas_call(
        functools.partial(attention_kernel, rows_per_block),
        out_shape=jax.ShapeDtypeStruct(
            (block_count, rows_per_block, heads * HEAD_SIZE), jnp.bfloat16
        ),
        in_specs=[pl.BlockSpec(memory_space=pltpu.SMEM)] * 2
        + [pl.BlockSpec(memory_space=pltpu.VMEM)] * 3,
        out_specs=pl.BlockSpec(memory_space=pltpu.VMEM),
        scratch_shapes=[
            pltpu.VMEM((slots, PAGE, 2 * HEAD_SIZE), jnp.bfloat16),
            pltpu.VMEM((slots, VROWS, PAGE), jnp.bfloat16),
            pltpu.VMEM((HEAD_SIZE, width), jnp.float32),
        ],
        compiler_params=pltpu.CompilerParams(vmem_limit_bytes=40 * 1024 * 1024),
        name="attend",
    )(bounds, where_from, gathered, fresh, query)
    attended = attended.reshape(row_count, heads * HEAD_SIZE)
    part = row_count // tensor_count
    columns = out_weight.shape[1] // tensor_count
    blocks = attended.reshape(tensor_count, part, heads * HEAD_SIZE)
    blocks = lax.all_to_all(blocks, "tensor", 0, 0)
    whole_rows = jnp.transpose(blocks, (1, 0, 2)).reshape(part, tensor_count * heads * HEAD_SIZE)
    made = jnp.dot(whole_rows, out_weight, preferred_element_type=jnp.float32).astype(jnp.bfloat16)
    made = jnp.transpose(made.reshape(part, tensor_count, columns), (1, 0, 2))
    return lax.all_to_all(made, "tensor", 0, 0).reshape(row_count, columns)


def solution(mesh):
    return jax.shard_map(
        body,
        mesh=mesh,
        in_specs=(
            P("seq", None),
            P(),
            P(None, "tensor"),
            P(),
            P(),
            P("seq", None, None, None),
            P(),
            P(),
            P(),
        ),
        out_specs=P("seq", "tensor"),
        check_vma=False,
    )
```

```python
import functools
import math

import jax
import jax.numpy as jnp
from jax import lax
from jax.experimental import pallas as pl
from jax.experimental.pallas import tpu as pltpu
from jax.sharding import PartitionSpec as P

QUERY_HEADS = 32
KEY_VALUE_HEADS = 4
HEAD_SIZE = 64
WINDOW_LENGTH = 2048
DEVICE_REQUESTS = 5
PPG = 64
WP = 16
PAGE = 128
VROWS = 80
MASKED_SCORE = -1e30
SCALE = HEAD_SIZE ** (-0.5) * math.log2(math.e)


def normalize(tokens, norm_gain):
    widened = tokens.astype(jnp.float32)
    factor = lax.rsqrt(jnp.mean(widened * widened, axis=-1, keepdims=True) + 1e-05)
    return (widened * factor * norm_gain).astype(jnp.bfloat16)


def lookup_rows(table, wanted):
    matches = wanted[:, None] == lax.iota(jnp.int32, table.shape[0])[None, :]
    return jnp.sum(jnp.where(matches[:, :, None], table[None, :, :], 0), axis=1)


def pack_kernel(count, slot_ref, cache_ref, out_ref, sems):
    for i in range(count):
        pltpu.make_async_copy(
            cache_ref.at[slot_ref[i], slot_ref[count]], out_ref.at[i], sems.at[i]
        ).start()
    for i in range(count):
        pltpu.make_async_copy(cache_ref.at[0, 0], out_ref.at[i], sems.at[i]).wait()


def attention_kernel(
    rows_per_block, bounds_ref, page_ref, pages_ref, fresh_ref, q_ref, out_ref, kv, vt, item_block, item_request
):
    block_count, _, width = q_ref.shape
    fresh_count = fresh_ref.shape[0]
    prefix_pages = DEVICE_REQUESTS * WP
    vt[:, HEAD_SIZE:, :] = jnp.ones((vt.shape[0], VROWS - HEAD_SIZE, PAGE), jnp.bfloat16)

    out_ref[...] = jnp.zeros_like(out_ref)

    def place(slot, page):
        kv[slot] = page
        vt[slot, :HEAD_SIZE, :] = jnp.transpose(page)[HEAD_SIZE:]

    def fill(i, carry):
        place(i, pages_ref[page_ref[i]])
        return carry

    lax.fori_loop(0, prefix_pages, fill, 0, unroll=4)
    for i in range(fresh_count):
        place(prefix_pages + i, fresh_ref[i])

    key_index = lax.broadcasted_iota(jnp.int32, (PAGE, width), 0)
    lane_row = lax.broadcasted_iota(jnp.int32, (1, width), 1) % rows_per_block

    block_row = lax.broadcasted_iota(jnp.int32, (rows_per_block, 1), 0)
    heads = width // rows_per_block

    def group(slots, masks, query, top, total):
        scores = []
        for slot, mask in zip(slots, masks):
            one = jnp.dot(kv[slot], query, preferred_element_type=jnp.float32) * SCALE
            scores.append(one if mask is None else jnp.where(mask, one, MASKED_SCORE))
        peak = functools.reduce(jnp.maximum, scores)
        peak = jnp.max(peak, axis=0, keepdims=True)
        new_top = peak if top is None else jnp.maximum(top, peak)
        weights = jnp.concatenate(
            [jnp.exp2(one - new_top).astype(jnp.bfloat16) for one in scores], axis=0
        )
        values = jnp.concatenate([vt[slot] for slot in slots], axis=1)
        added = jnp.dot(values, weights, preferred_element_type=jnp.float32)
        if total is not None:
            added = added + total * jnp.exp2(top - new_top)
        return new_top, added

    def one_item(request, block):
        first_row = block * rows_per_block
        start = bounds_ref[request]
        query = q_ref[block]
        row = lane_row + first_row
        position = row - start
        first_fresh = start // PAGE
        last_fresh = first_row // PAGE
        first_page = (jnp.maximum(first_row - start, 0) + 1) // PAGE
        base = request * WP
        inside = 14 - first_page
        several = last_fresh > first_fresh

        def plain(u):
            wanted = prefix_pages + first_fresh + 1 + (u - inside)
            return jnp.where(u < inside, base + first_page + 2 + u, wanted)

        count = inside + jnp.maximum(last_fresh - first_fresh - 1, 0)
        slots = [
            base + first_page,
            base + first_page + 1,
            prefix_pages + first_fresh,
            prefix_pages + last_fresh,
            plain(12),
            jnp.where(count > 13, plain(13), base),
        ]
        fresh_low = start - first_fresh * PAGE
        last_high = jnp.where(several, row - last_fresh * PAGE, -1)
        masks = [
            key_index > position - first_page * PAGE,
            key_index > position - (first_page + 1) * PAGE,
            (key_index <= row - first_fresh * PAGE) & (key_index >= fresh_low),
            key_index <= last_high,
            None,
            key_index < jnp.where(count > 13, PAGE, 0),
        ]
        top, total = group(slots, masks, query, None, None)
        for part in range(2):
            slots = [plain(part * 6 + u) for u in range(6)]
            top, total = group(slots, [None] * 6, query, top, total)
        result = total[:HEAD_SIZE] / total[HEAD_SIZE : HEAD_SIZE + 1]
        turned = jnp.transpose(result)
        pieces = [turned[h * rows_per_block : (h + 1) * rows_per_block] for h in range(heads)]
        return jnp.concatenate(pieces, axis=1)

    def store_item(request, block, live, made):
        row = block_row + block * rows_per_block
        end = jnp.where(live, bounds_ref[DEVICE_REQUESTS + request], 0)
        mine = (row >= bounds_ref[request]) & (row < end)
        kept = out_ref[block].astype(jnp.float32)
        out_ref[block] = jnp.where(mine, made, kept).astype(jnp.bfloat16)

    def list_block(block, count):
        first_row = block * rows_per_block
        first = 0
        last = -1
        for r in range(DEVICE_REQUESTS):
            first = first + (bounds_ref[DEVICE_REQUESTS + r] <= first_row).astype(jnp.int32)
            last = last + (bounds_ref[r] < first_row + rows_per_block).astype(jnp.int32)

        def add(request, count):
            item_block[count] = block
            item_request[count] = request
            return count + 1

        return lax.fori_loop(first, last + 1, add, count)

    count = lax.fori_loop(0, block_count, list_block, 0)
    item_block[count] = 0
    item_request[count] = 0

    def pair(step, carry):
        items = [(item_request[2 * step + i], item_block[2 * step + i]) for i in range(2)]
        results = [one_item(*item) for item in items]
        for i in range(2):
            store_item(*items[i], 2 * step + i < count, results[i])
        return carry

    lax.fori_loop(0, (count + 1) // 2, pair, 0)


def body(
    tokens,
    norm_gain,
    query_weight,
    key_value_matrix,
    out_weight,
    cache_pages,
    page_table,
    request_lengths,
    request_groups,
):
    seq_count = lax.axis_size("seq")
    seq_index = lax.axis_index("seq")
    tensor_index = lax.axis_index("tensor")
    tensor_count = lax.axis_size("tensor")
    row_count = tokens.shape[0]
    heads = query_weight.shape[1] // HEAD_SIZE
    key_value_head = tensor_index * heads // (QUERY_HEADS // KEY_VALUE_HEADS)
    group_count = page_table.shape[0]
    per_owner = WP // seq_count
    pages_here = cache_pages.shape[0]
    send_count = group_count * per_owner

    tail_ids = page_table[:, PPG - WP :]
    holder = tail_ids // pages_here
    local_slot = tail_ids % pages_here
    earlier = lax.iota(jnp.int32, WP)[:, None] > lax.iota(jnp.int32, WP)[None, :]
    same_owner = holder[:, :, None] == holder[:, None, :]
    tail_rank = jnp.sum((same_owner & earlier[None, :, :]).astype(jnp.int32), axis=2)
    tail_hit = (holder == seq_index)[:, :, None] & (
        tail_rank[:, :, None] == lax.iota(jnp.int32, per_owner)[None, None, :]
    )
    tail_pick = jnp.sum(jnp.where(tail_hit, local_slot[:, :, None], 0), axis=1).reshape(-1)
    packed = pl.pallas_call(
        functools.partial(pack_kernel, send_count),
        out_shape=jax.ShapeDtypeStruct((send_count, PAGE, 2 * HEAD_SIZE), jnp.bfloat16),
        in_specs=[
            pl.BlockSpec(memory_space=pltpu.SMEM),
            pl.BlockSpec(memory_space=pl.ANY),
        ],
        out_specs=pl.BlockSpec(memory_space=pltpu.VMEM),
        scratch_shapes=[pltpu.SemaphoreType.DMA((send_count,))],
        name="pack_pages",
    )(jnp.concatenate([tail_pick, key_value_head[None].astype(jnp.int32)]), cache_pages)
    gathered = lax.all_gather(packed, "seq", axis=0, tiled=True)

    normed = normalize(tokens, norm_gain)
    query_rows = jnp.dot(normed, query_weight, preferred_element_type=jnp.float32).astype(
        jnp.bfloat16
    )
    head_weight = lax.dynamic_index_in_dim(key_value_matrix, key_value_head, 1, keepdims=False)
    fresh = jnp.dot(normed, head_weight, preferred_element_type=jnp.float32).astype(jnp.bfloat16)
    fresh = fresh.reshape(row_count // PAGE, PAGE, 2 * HEAD_SIZE)
    rows_per_block = min(PAGE, 256 // heads)
    block_count = row_count // rows_per_block
    width = heads * rows_per_block
    query = query_rows.reshape(block_count, rows_per_block, heads, HEAD_SIZE)
    query = jnp.transpose(query, (0, 3, 2, 1)).reshape(block_count, HEAD_SIZE, width)
    query = jnp.concatenate([query, jnp.zeros_like(query)], axis=1)

    lengths = lax.dynamic_slice_in_dim(
        request_lengths, seq_index * DEVICE_REQUESTS, DEVICE_REQUESTS
    )
    groups = lax.dynamic_slice_in_dim(
        request_groups, seq_index * DEVICE_REQUESTS, DEVICE_REQUESTS
    )
    ends = jnp.cumsum(lengths)
    bounds = jnp.concatenate([ends - lengths, ends])
    where_from = (
        lookup_rows(holder, groups) * send_count
        + groups[:, None] * per_owner
        + lookup_rows(tail_rank, groups)
    ).reshape(-1)
    slots = DEVICE_REQUESTS * WP + row_count // PAGE
    attended = pl.pallas_call(
        functools.partial(attention_kernel, rows_per_block),
        out_shape=jax.ShapeDtypeStruct(
            (block_count, rows_per_block, heads * HEAD_SIZE), jnp.bfloat16
        ),
        in_specs=[pl.BlockSpec(memory_space=pltpu.SMEM)] * 2
        + [pl.BlockSpec(memory_space=pltpu.VMEM)] * 3,
        out_specs=pl.BlockSpec(memory_space=pltpu.VMEM),
        scratch_shapes=[
            pltpu.VMEM((slots, PAGE, 2 * HEAD_SIZE), jnp.bfloat16),
            pltpu.VMEM((slots, VROWS, PAGE), jnp.bfloat16),
            pltpu.SMEM((block_count + DEVICE_REQUESTS + 1,), jnp.int32),
            pltpu.SMEM((block_count + DEVICE_REQUESTS + 1,), jnp.int32),
        ],
        compiler_params=pltpu.CompilerParams(vmem_limit_bytes=40 * 1024 * 1024),
        name="attend",
    )(bounds, where_from, gathered, fresh, query)
    attended = attended.reshape(row_count, heads * HEAD_SIZE)
    part = row_count // tensor_count
    columns = out_weight.shape[1] // tensor_count
    blocks = attended.reshape(tensor_count, part, heads * HEAD_SIZE)
    blocks = lax.all_to_all(blocks, "tensor", 0, 0)
    whole_rows = jnp.transpose(blocks, (1, 0, 2)).reshape(part, tensor_count * heads * HEAD_SIZE)
    made = jnp.dot(whole_rows, out_weight, preferred_element_type=jnp.float32).astype(jnp.bfloat16)
    made = jnp.transpose(made.reshape(part, tensor_count, columns), (1, 0, 2))
    return lax.all_to_all(made, "tensor", 0, 0).reshape(row_count, columns)


def solution(mesh):
    return jax.shard_map(
        body,
        mesh=mesh,
        in_specs=(
            P("seq", None),
            P(),
            P(None, "tensor"),
            P(),
            P(),
            P("seq", None, None, None),
            P(),
            P(),
            P(),
        ),
        out_specs=P("seq", "tensor"),
        check_vma=False,
    )
```

```python
import functools
import math

import jax
import jax.numpy as jnp
from jax import lax
from jax.experimental import pallas as pl
from jax.experimental.pallas import tpu as pltpu
from jax.sharding import PartitionSpec as P

QUERY_HEADS = 32
KEY_VALUE_HEADS = 4
HEAD_SIZE = 64
WINDOW_LENGTH = 2048
DEVICE_REQUESTS = 5
PPG = 64
WP = 16
PAGE = 128
VROWS = 80
MASKED_SCORE = -1e30
SCALE = HEAD_SIZE ** (-0.5) * math.log2(math.e)


def normalize(tokens, norm_gain):
    widened = tokens.astype(jnp.float32)
    factor = lax.rsqrt(jnp.mean(widened * widened, axis=-1, keepdims=True) + 1e-05)
    return (widened * factor * norm_gain).astype(jnp.bfloat16)


def lookup_rows(table, wanted):
    matches = wanted[:, None] == lax.iota(jnp.int32, table.shape[0])[None, :]
    return jnp.sum(jnp.where(matches[:, :, None], table[None, :, :], 0), axis=1)


def pack_kernel(count, slot_ref, cache_ref, out_ref, sems):
    for i in range(count):
        pltpu.make_async_copy(
            cache_ref.at[slot_ref[i], slot_ref[count]], out_ref.at[i], sems.at[i]
        ).start()
    for i in range(count):
        pltpu.make_async_copy(cache_ref.at[0, 0], out_ref.at[i], sems.at[i]).wait()


def attention_kernel(
    rows_per_block, bounds_ref, page_ref, pages_ref, fresh_ref, q_ref, out_ref, kv, vt, item_block, item_request
):
    block_count, _, width = q_ref.shape
    fresh_count = fresh_ref.shape[0]
    prefix_pages = DEVICE_REQUESTS * WP
    vt[:, HEAD_SIZE:, :] = jnp.ones((vt.shape[0], VROWS - HEAD_SIZE, PAGE), jnp.bfloat16)

    out_ref[...] = jnp.zeros_like(out_ref)

    def place(slot, page):
        kv[slot] = page
        vt[slot, :HEAD_SIZE, :] = jnp.transpose(page)[HEAD_SIZE:]

    def fill(i, carry):
        place(i, pages_ref[page_ref[i]])
        return carry

    lax.fori_loop(0, prefix_pages, fill, 0, unroll=16)
    for i in range(fresh_count):
        place(prefix_pages + i, fresh_ref[i])

    key_index = lax.broadcasted_iota(jnp.int32, (PAGE, width), 0)
    lane_row = lax.broadcasted_iota(jnp.int32, (1, width), 1) % rows_per_block

    block_row = lax.broadcasted_iota(jnp.int32, (rows_per_block, 1), 0)
    heads = width // rows_per_block

    def group(slots, masks, query, top, total):
        scores = []
        for slot, mask in zip(slots, masks):
            one = jnp.dot(kv[slot], query, preferred_element_type=jnp.float32) * SCALE
            scores.append(one if mask is None else jnp.where(mask, one, MASKED_SCORE))
        peak = functools.reduce(jnp.maximum, scores)
        peak = jnp.max(peak, axis=0, keepdims=True)
        new_top = peak if top is None else jnp.maximum(top, peak)
        weights = jnp.concatenate(
            [jnp.exp2(one - new_top).astype(jnp.bfloat16) for one in scores], axis=0
        )
        values = jnp.concatenate([vt[slot] for slot in slots], axis=1)
        added = jnp.dot(values, weights, preferred_element_type=jnp.float32)
        if total is not None:
            added = added + total * jnp.exp2(top - new_top)
        return new_top, added

    def one_item(request, block):
        first_row = block * rows_per_block
        start = bounds_ref[request]
        query = q_ref[block]
        row = lane_row + first_row
        position = row - start
        first_fresh = start // PAGE
        last_fresh = first_row // PAGE
        first_page = (jnp.maximum(first_row - start, 0) + 1) // PAGE
        base = request * WP
        inside = 14 - first_page
        several = last_fresh > first_fresh

        def plain(u):
            wanted = prefix_pages + first_fresh + 1 + (u - inside)
            return jnp.where(u < inside, base + first_page + 2 + u, wanted)

        count = inside + jnp.maximum(last_fresh - first_fresh - 1, 0)
        slots = [
            base + first_page,
            base + first_page + 1,
            prefix_pages + first_fresh,
            prefix_pages + last_fresh,
            plain(12),
            jnp.where(count > 13, plain(13), base),
        ]
        fresh_low = start - first_fresh * PAGE
        last_high = jnp.where(several, row - last_fresh * PAGE, -1)
        masks = [
            key_index > position - first_page * PAGE,
            key_index > position - (first_page + 1) * PAGE,
            (key_index <= row - first_fresh * PAGE) & (key_index >= fresh_low),
            key_index <= last_high,
            None,
            key_index < jnp.where(count > 13, PAGE, 0),
        ]
        top, total = group(slots, masks, query, None, None)
        for part in range(1):
            slots = [plain(part * 12 + u) for u in range(12)]
            top, total = group(slots, [None] * 12, query, top, total)
        result = total[:HEAD_SIZE] / total[HEAD_SIZE : HEAD_SIZE + 1]
        turned = jnp.transpose(result)
        pieces = [turned[h * rows_per_block : (h + 1) * rows_per_block] for h in range(heads)]
        return jnp.concatenate(pieces, axis=1)

    def store_item(request, block, live, made):
        row = block_row + block * rows_per_block
        end = jnp.where(live, bounds_ref[DEVICE_REQUESTS + request], 0)
        mine = (row >= bounds_ref[request]) & (row < end)
        kept = out_ref[block].astype(jnp.float32)
        out_ref[block] = jnp.where(mine, made, kept).astype(jnp.bfloat16)

    def list_block(block, count):
        first_row = block * rows_per_block
        first = 0
        last = -1
        for r in range(DEVICE_REQUESTS):
            first = first + (bounds_ref[DEVICE_REQUESTS + r] <= first_row).astype(jnp.int32)
            last = last + (bounds_ref[r] < first_row + rows_per_block).astype(jnp.int32)

        def add(request, count):
            item_block[count] = block
            item_request[count] = request
            return count + 1

        return lax.fori_loop(first, last + 1, add, count)

    count = lax.fori_loop(0, block_count, list_block, 0)
    item_block[count] = 0
    item_request[count] = 0

    def pair(step, carry):
        items = [(item_request[2 * step + i], item_block[2 * step + i]) for i in range(2)]
        results = [one_item(*item) for item in items]
        for i in range(2):
            store_item(*items[i], 2 * step + i < count, results[i])
        return carry

    lax.fori_loop(0, (count + 1) // 2, pair, 0)


def body(
    tokens,
    norm_gain,
    query_weight,
    key_value_matrix,
    out_weight,
    cache_pages,
    page_table,
    request_lengths,
    request_groups,
):
    seq_count = lax.axis_size("seq")
    seq_index = lax.axis_index("seq")
    tensor_index = lax.axis_index("tensor")
    tensor_count = lax.axis_size("tensor")
    row_count = tokens.shape[0]
    heads = query_weight.shape[1] // HEAD_SIZE
    key_value_head = tensor_index * heads // (QUERY_HEADS // KEY_VALUE_HEADS)
    group_count = page_table.shape[0]
    per_owner = WP // seq_count
    pages_here = cache_pages.shape[0]
    send_count = group_count * per_owner

    tail_ids = page_table[:, PPG - WP :]
    holder = tail_ids // pages_here
    local_slot = tail_ids % pages_here
    earlier = lax.iota(jnp.int32, WP)[:, None] > lax.iota(jnp.int32, WP)[None, :]
    same_owner = holder[:, :, None] == holder[:, None, :]
    tail_rank = jnp.sum((same_owner & earlier[None, :, :]).astype(jnp.int32), axis=2)
    tail_hit = (holder == seq_index)[:, :, None] & (
        tail_rank[:, :, None] == lax.iota(jnp.int32, per_owner)[None, None, :]
    )
    tail_pick = jnp.sum(jnp.where(tail_hit, local_slot[:, :, None], 0), axis=1).reshape(-1)
    packed = pl.pallas_call(
        functools.partial(pack_kernel, send_count),
        out_shape=jax.ShapeDtypeStruct((send_count, PAGE, 2 * HEAD_SIZE), jnp.bfloat16),
        in_specs=[
            pl.BlockSpec(memory_space=pltpu.SMEM),
            pl.BlockSpec(memory_space=pl.ANY),
        ],
        out_specs=pl.BlockSpec(memory_space=pltpu.VMEM),
        scratch_shapes=[pltpu.SemaphoreType.DMA((send_count,))],
        name="pack_pages",
    )(jnp.concatenate([tail_pick, key_value_head[None].astype(jnp.int32)]), cache_pages)
    gathered = lax.all_gather(packed, "seq", axis=0, tiled=True)

    normed = normalize(tokens, norm_gain)
    query_rows = jnp.dot(normed, query_weight, preferred_element_type=jnp.float32).astype(
        jnp.bfloat16
    )
    head_weight = lax.dynamic_index_in_dim(key_value_matrix, key_value_head, 1, keepdims=False)
    fresh = jnp.dot(normed, head_weight, preferred_element_type=jnp.float32).astype(jnp.bfloat16)
    fresh = fresh.reshape(row_count // PAGE, PAGE, 2 * HEAD_SIZE)
    rows_per_block = min(PAGE, 256 // heads)
    block_count = row_count // rows_per_block
    width = heads * rows_per_block
    query = query_rows.reshape(block_count, rows_per_block, heads, HEAD_SIZE)
    query = jnp.transpose(query, (0, 3, 2, 1)).reshape(block_count, HEAD_SIZE, width)
    query = jnp.concatenate([query, jnp.zeros_like(query)], axis=1)

    lengths = lax.dynamic_slice_in_dim(
        request_lengths, seq_index * DEVICE_REQUESTS, DEVICE_REQUESTS
    )
    groups = lax.dynamic_slice_in_dim(
        request_groups, seq_index * DEVICE_REQUESTS, DEVICE_REQUESTS
    )
    ends = jnp.cumsum(lengths)
    bounds = jnp.concatenate([ends - lengths, ends])
    where_from = (
        lookup_rows(holder, groups) * send_count
        + groups[:, None] * per_owner
        + lookup_rows(tail_rank, groups)
    ).reshape(-1)
    slots = DEVICE_REQUESTS * WP + row_count // PAGE
    attended = pl.pallas_call(
        functools.partial(attention_kernel, rows_per_block),
        out_shape=jax.ShapeDtypeStruct(
            (block_count, rows_per_block, heads * HEAD_SIZE), jnp.bfloat16
        ),
        in_specs=[pl.BlockSpec(memory_space=pltpu.SMEM)] * 2
        + [pl.BlockSpec(memory_space=pltpu.VMEM)] * 3,
        out_specs=pl.BlockSpec(memory_space=pltpu.VMEM),
        scratch_shapes=[
            pltpu.VMEM((slots, PAGE, 2 * HEAD_SIZE), jnp.bfloat16),
            pltpu.VMEM((slots, VROWS, PAGE), jnp.bfloat16),
            pltpu.SMEM((block_count + DEVICE_REQUESTS + 1,), jnp.int32),
            pltpu.SMEM((block_count + DEVICE_REQUESTS + 1,), jnp.int32),
        ],
        compiler_params=pltpu.CompilerParams(vmem_limit_bytes=40 * 1024 * 1024),
        name="attend",
    )(bounds, where_from, gathered, fresh, query)
    attended = attended.reshape(row_count, heads * HEAD_SIZE)
    part = row_count // tensor_count
    columns = out_weight.shape[1] // tensor_count
    blocks = attended.reshape(tensor_count, part, heads * HEAD_SIZE)
    blocks = lax.all_to_all(blocks, "tensor", 0, 0)
    whole_rows = jnp.transpose(blocks, (1, 0, 2)).reshape(part, tensor_count * heads * HEAD_SIZE)
    made = jnp.dot(whole_rows, out_weight, preferred_element_type=jnp.float32).astype(jnp.bfloat16)
    made = jnp.transpose(made.reshape(part, tensor_count, columns), (1, 0, 2))
    return lax.all_to_all(made, "tensor", 0, 0).reshape(row_count, columns)


def solution(mesh):
    return jax.shard_map(
        body,
        mesh=mesh,
        in_specs=(
            P("seq", None),
            P(),
            P(None, "tensor"),
            P(),
            P(),
            P("seq", None, None, None),
            P(),
            P(),
            P(),
        ),
        out_specs=P("seq", "tensor"),
        check_vma=False,
    )
```
